128 devices in a mesh: env: 8 (over x, core), wf: 16 (over y, z).
Axes of the slice: x: 4, y: 4, z: 4, core: 2. Of those that a mesh axis runs over, the one named last changes fastest.
Arguments:
- wavefunction: bfloat16 [256, 256, 256], P('wf'), may hold values from -6 to 6
- left_env: bfloat16 [32, 256, 256, 256], P('env', 'wf'), may hold values from -0.375 to 0.375
- right_env: bfloat16 [32, 256, 256, 256], P('env', 'wf'), may hold values from -0.0625 to 0.0625
- term_class: int32 [32], P('env'), may hold values from 0 to 4
- sector_sizes: int32 [2, 256], P(None, 'wf'), may hold values from 128 to 256, as said below
- source_table: int32 [5, 256], replicated, may hold values from 0 to 255, as said below
Outputs:
- product_wf: bfloat16 [256, 256, 256], P(('wf', 'env'))
The draws below stay inside these ranges and needn't reach their ends.
Inputs may be any that keep to these rules, and one draw needn't show every extreme that they name: `sector_sizes`: both rows reach 128 and 256 on some sector. `source_table`: each row is a permutation of the 256 sectors. Sectors lie in order, 16 to an index of wf; for every class, the 16 target sectors of one index of wf are reached from exactly one sector of each index of wf.
All inputs are finite; a program needn't handle non-finite values.
Results may differ from the reference program's by a relative error of at most 0.0049.
Values may be sent and summed in bfloat16 or wider, within the bound.
A program may use at most 128 MiB of HBM per device.

```python
import jax
import jax.numpy as jnp
from jax import lax

BLOCK = 256
CLASSES = 5
SECT_DEV = 16
TERMS = 32
SECTORS = 256


def draw_sector_sizes(key, part):
    key = jax.random.fold_in(key, 11)
    first_key, second_key = jax.random.split(key)
    sector_len = jax.random.randint(first_key, (2, SECTORS), BLOCK // 2, BLOCK + 1)
    positions = jax.random.permutation(second_key, SECTORS)
    sector_len = sector_len.at[:, positions[0]].set(BLOCK)
    sector_len = sector_len.at[:, positions[1]].set(BLOCK // 2)
    return sector_len.astype(jnp.int32)


def draw_source_table(key, part):
    key = jax.random.fold_in(key, 23)
    wf_devices = SECTORS // SECT_DEV
    per_pair = SECT_DEV // wf_devices
    first_key, second_key = jax.random.split(key)
    offset_perm = jax.vmap(lambda one_key: jax.random.permutation(one_key, SECT_DEV))(jax.random.split(first_key, CLASSES * wf_devices))
    offset_perm = offset_perm.reshape(CLASSES, wf_devices, SECT_DEV)
    slot_perm = jax.vmap(lambda one_key: jax.random.permutation(one_key, SECT_DEV))(jax.random.split(second_key, CLASSES * wf_devices))
    slot_perm = slot_perm.reshape(CLASSES, wf_devices, SECT_DEV)
    dest_dev = jnp.arange(wf_devices)[None, :, None]
    from_dev = jnp.mod(dest_dev + offset_perm, wf_devices)
    arrival = jnp.mod(-offset_perm, wf_devices) * per_pair + offset_perm // wf_devices
    class_ids = jnp.arange(CLASSES)[:, None, None]
    from_slot = slot_perm[class_ids, from_dev, arrival]
    return (from_dev * SECT_DEV + from_slot).reshape(CLASSES, SECTORS).astype(jnp.int32)


def set_ends(entries, stream_key, smallest, largest):
    spot = [jax.random.randint(jax.random.fold_in(stream_key, axis), (), 0, length) for axis, length in enumerate(entries.shape)]
    longest = entries.shape.index(max(entries.shape))
    next_to = spot[:longest] + [(spot[longest] + 1) % entries.shape[longest]] + spot[longest + 1:]
    return entries.at[tuple(spot)].set(smallest).at[tuple(next_to)].set(largest)


def block_levels(own_key, extent, shards, smallest, high):
    def one(axis_at, parts):
        heights = jax.random.uniform(jax.random.fold_in(jax.random.fold_in(own_key, 6), axis_at), (parts,), jnp.float32, smallest / len(shards), high / len(shards))
        return jnp.repeat(jnp.exp(heights), extent[axis_at] // parts).reshape((-1,) + (1,) * (len(extent) - axis_at - 1))

    loudness = one(*shards[0])
    for cut in shards[1:]:
        loudness = loudness * one(*cut)
    return loudness


def noise(stream_key, dims, deviation, bound, cuts=(), kind=jnp.bfloat16):
    drawn = deviation * jax.random.normal(stream_key, dims, jnp.float32)
    if cuts:
        drawn = drawn * block_levels(stream_key, dims, cuts, -0.22, 0.18)
    return jnp.clip(drawn, -bound, bound).astype(kind)


def setup_inputs(seed: int = 0) -> dict:
    streams_of = jax.random.split(jax.random.key(seed), 7)
    return {
        "wavefunction": noise(streams_of[0], (SECTORS, BLOCK, BLOCK), 1.0, 6.0, ((0, 16),)),
        "left_env": noise(streams_of[1], (TERMS, SECTORS, BLOCK, BLOCK), BLOCK ** -0.5, 0.375, ((0, 8), (1, 16))),
        "right_env": noise(streams_of[2], (TERMS, SECTORS, BLOCK, BLOCK), (BLOCK * TERMS) ** -0.5, 0.0625, ((0, 8), (1, 16))),
        "term_class": set_ends(jax.random.randint(streams_of[3], (TERMS,), 0, CLASSES), jax.random.fold_in(streams_of[3], 1), 0, CLASSES - 1).astype(jnp.int32),
        "sector_sizes": draw_sector_sizes(jax.random.fold_in(streams_of[6], 71), 0),
        "source_table": draw_source_table(jax.random.fold_in(streams_of[6], 71), 0),
    }


def reference(wavefunction, left_env, right_env, term_class, sector_sizes, source_table):
    positions = jnp.arange(BLOCK)
    rows_ok = positions[None, :] < sector_sizes[0][:, None]
    cols_ok = positions[None, :] < sector_sizes[1][:, None]
    valid_mask = rows_ok[:, :, None] & cols_ok[:, None, :]
    masked = jnp.where(valid_mask, wavefunction, jnp.zeros((), jnp.bfloat16))

    def accumulate(running, inputs):
        left_block, right_block, class_id = inputs
        sources = jnp.take(source_table, class_id, axis=0)
        fetched = jnp.take(masked, sources, axis=0)
        partial_left = jnp.einsum("qab,qbc->qac", left_block.astype(jnp.float32), fetched.astype(jnp.float32)).astype(jnp.bfloat16)
        running = running + jnp.einsum("qac,qdc->qad", partial_left.astype(jnp.float32), right_block.astype(jnp.float32))
        return running, None

    initial = jnp.zeros((SECTORS, BLOCK, BLOCK), jnp.float32)
    combined, unused = lax.scan(accumulate, initial, (left_env, right_env, term_class))
    return jnp.where(valid_mask, combined, jnp.zeros((), combined.dtype)).astype(jnp.bfloat16)
```

```python
import jax
import jax.numpy as jnp
from jax import lax
from jax.experimental import pallas as pl
from jax.experimental.pallas import tpu as pltpu
from jax.sharding import PartitionSpec as P

MESH = pl.DeviceIdType.MESH
B = 256
HALF = B // 2
PIECE = HALF // 4
CLASSES = 5
GROUP = 16
TERMS = 4

COOP = (
    ((1, 1), (1, 0)),
    ((3, 3), (3, 0)),
    ((1, 3), (0, 3)),
    ((3, 1), (0, 1)),
    ((2, 1), (0, 1)),
    ((2, 3), (0, 3)),
    ((1, 2), (1, 0)),
    ((3, 2), (3, 0)),
    ((2, 2), None),
)
DIRECT = ((0, 1), (0, 3), (1, 0), (3, 0), (0, 2), (2, 0))
OFFSETS = tuple(o for o, _ in COOP) + DIRECT
NC, ND, NO = len(COOP), len(DIRECT), len(COOP) + len(DIRECT)
XORDER = (2, 1, 3, 0)


def body(slot, qinv, osrc, klass, sizes, wf_hbm, left_hbm, right_hbm, out, *scratch):
    recv = scratch[:NO]
    (wf, left, right, stage_c, transit, stage_d, partial, core_out, core_in, mine, x_out, x_in,
     load_sem, s1, r1, s2, r2, sd, rd, sx, rx, sf, rf, sc, rc, sp, rp, sr, rr) = scratch[NO:]
    e, w = lax.axis_index("env"), lax.axis_index("wf")
    x, c, y, z = e // 2, e % 2, w // 4, w % 4

    def dev(dx, dc, dy, dz):
        return (((x + dx) % 4) * 2 + (c + dc) % 2, ((y + dy) % 4) * 4 + (z + dz) % 4)

    def remote(src, dst, ssem, rsem, dx, dc, dy, dz):
        return pltpu.make_async_remote_copy(
            src_ref=src, dst_ref=dst, send_sem=ssem, recv_sem=rsem, device_id=dev(dx, dc, dy, dz), device_id_type=MESH)

    load_wf = pltpu.make_async_copy(wf_hbm, wf, load_sem.at[0])
    load_wf.start()
    barrier = pltpu.get_barrier_semaphore()
    partners = [(0, 1, 0, 0)] + [(d, 0, 0, 0) for d in (1, 2, 3)] + [(0, 0, d, 0) for d in (1, 2, 3)] + [(0, 0, 0, d) for d in (1, 2, 3)]
    for p in partners:
        pl.semaphore_signal(barrier, inc=1, device_id=dev(*p), device_id_type=MESH)
    load_wf.wait()
    load_left = pltpu.make_async_copy(left_hbm, left, load_sem.at[1])
    load_right = pltpu.make_async_copy(right_hbm, right, load_sem.at[2])
    load_left.start()
    load_right.start()

    rows = lax.broadcasted_iota(jnp.int32, (B, B), 0)
    cols = lax.broadcasted_iota(jnp.int32, (B, B), 1)

    @pl.loop(0, GROUP)
    def _(q):
        keep = (rows < sizes[0, q]) & (cols < sizes[1, q])
        wf[q] = jnp.where(keep, wf[q].astype(jnp.float32), 0.0).astype(jnp.bfloat16)

    half = pl.multiple_of(c * HALF, HALF)
    piece = pl.multiple_of(c * HALF + x * PIECE, PIECE)
    prev_piece = pl.multiple_of(c * HALF + ((x + 3) % 4) * PIECE, PIECE)
    next_piece = pl.multiple_of(c * HALF + ((x + 1) % 4) * PIECE, PIECE)
    low = PIECE // 2

    def target(o):
        return ((y + o[0]) % 4) * 4 + (z + o[1]) % 4

    def stage(dst, o, first, count):
        @pl.loop(0, CLASSES)
        def _(k):
            dst[k] = wf[slot[k, target(o)], pl.ds(first, count)]

    def leg1(i):
        o, hop = COOP[i]
        if hop is None:
            hop = (2 * (1 - c), 2 * c)
        return remote(stage_c.at[i], transit.at[i], s1.at[i], r1.at[i], 0, 0, *hop)

    def leg2(i):
        o, hop = COOP[i]
        hop = (2 * c, 2 * (1 - c)) if hop is None else ((o[0] - hop[0]) % 4, (o[1] - hop[1]) % 4)
        return remote(transit.at[i], recv[i].at[:, pl.ds(piece, PIECE)], s2.at[i], r2.at[i], 0, 0, *hop)

    def direct(i):
        return remote(stage_d.at[i], recv[NC + i].at[:, pl.ds(half, HALF)], sd.at[i], rd.at[i], 0, 0, *DIRECT[i])

    def share(i, side):
        part = recv[i].at[:, pl.ds(piece, PIECE)]
        return remote(part, part, sx.at[side, i], rx.at[side, i], 1 if side == 0 else 3, 0, 0, 0)

    def forward(i, side):
        first = prev_piece if side == 0 else next_piece + low
        part = recv[i].at[:, pl.ds(pl.multiple_of(first, low), low)]
        return remote(part, part, sf.at[side, i], rf.at[side, i], 1 if side == 0 else 3, 0, 0, 0)

    def across(i):
        part = recv[i].at[:, pl.ds(half, HALF)]
        return remote(part, part, sc.at[i], rc.at[i], 0, 1, 0, 0)

    def first_product(i):
        o = OFFSETS[i]

        @pl.loop(0, TERMS)
        def _(k):
            kind = klass[k]
            at = o[0] * 4 + o[1]
            got = lax.dot_general(left[k, qinv[kind, at]], recv[i][kind], (((1,), (0,)), ((), ())), preferred_element_type=jnp.float32)
            partial[k, at] = got.astype(jnp.bfloat16)

    for i in range(NC):
        stage(stage_c.at[i], COOP[i][0], piece, PIECE)
    pl.semaphore_wait(barrier, len(partners))
    for i in range(NC):
        leg1(i).start()
    for i in range(ND):
        stage(stage_d.at[i], DIRECT[i], half, HALF)

    for i in range(4):
        leg1(i).wait_recv()
        leg2(i).start()
    for i in range(4):
        direct(i).start()
    for i in range(4, NC):
        leg1(i).wait_recv()
        leg2(i).start()
    for i in range(4, ND):
        direct(i).start()

    load_left.wait()

    @pl.loop(0, TERMS)
    def _(k):
        kind = klass[k]
        got = lax.dot_general(left[k, qinv[kind, 0]], wf[slot[kind, target((0, 0))]], (((1,), (0,)), ((), ())), preferred_element_type=jnp.float32)
        partial[k, 0] = got.astype(jnp.bfloat16)

    def step_share(i):
        leg2(i).wait_recv()
        share(i, 0).start()
        share(i, 1).start()

    def step_forward(i):
        for side in (0, 1):
            share(i, side).wait_recv()
            forward(i, side).start()

    def step_across(i):
        for side in (0, 1):
            forward(i, side).wait_recv()
        across(i).start()

    def step_direct(i):
        direct(i).wait_recv()
        across(NC + i).start()

    def step_product(i):
        across(i).wait_recv()
        first_product(i)

    for t in range(NC + 4):
        if t < NC:
            step_share(t)
        if 0 <= t - 1 < NC:
            step_forward(t - 1)
        if 0 <= t - 2 < NC:
            step_across(t - 2)
        if 0 <= t - 4 < NC:
            step_product(t - 4)
        if 0 <= t - 5 < ND:
            step_direct(t - 5)
        if 0 <= t - 7 < ND:
            step_product(NC + t - 7)
    load_right.wait()

    def second_product(q):
        total = jnp.zeros((B, B), jnp.float32)
        for k in range(TERMS):
            total += lax.dot_general(partial[k, osrc[klass[k], q]], right[k, q], (((1,), (1,)), ((), ())), preferred_element_type=jnp.float32)
        return total

    def to_core(n):
        return remote(core_out.at[n], core_in.at[n], sp.at[n], rp.at[n], 0, 1, 0, 0)

    def to_plane(n):
        return remote(x_out.at[n], x_in.at[n], sr.at[n], rr.at[n], XORDER[n], 0, 0, 0)

    def theirs(n):
        first = ((x + XORDER[n]) % 4) * 4 + 2 * (1 - c)

        @pl.loop(0, 2)
        def _(j):
            core_out[n, j] = second_product(first + j)

        to_core(n).start()

    def ours(n):
        first = ((x + XORDER[n]) % 4) * 4 + 2 * c

        @pl.loop(0, 2)
        def _(j):
            mine[n, j] = second_product(first + j)

    def send_sum(n):
        to_core(n).wait_recv()

        @pl.loop(0, 2)
        def _(j):
            x_out[n, j] = (mine[n, j] + core_in[n, j]).astype(jnp.bfloat16)

        to_plane(n).start()

    theirs(0)
    theirs(1)
    ours(0)
    send_sum(0)
    ours(1)
    send_sum(1)
    theirs(2)
    theirs(3)
    ours(2)
    send_sum(2)
    ours(3)
    to_core(3).wait_recv()
    for n in (1, 2, 0):
        to_plane(n).wait_recv()

    @pl.loop(0, 2)
    def _(j):
        q = 4 * x + 2 * c + j
        total = mine[3, j] + core_in[3, j]
        for n in range(3):
            total += x_in[n, j].astype(jnp.float32)
        keep = (rows < sizes[0, q]) & (cols < sizes[1, q])
        out[j] = jnp.where(keep, total, 0.0).astype(jnp.bfloat16)

    for i in range(NC):
        leg1(i).wait_send()
        leg2(i).wait_send()
        for side in (0, 1):
            share(i, side).wait_send()
            forward(i, side).wait_send()
    for i in range(ND):
        direct(i).wait_send()
    for i in range(NO):
        across(i).wait_send()
    for n in range(4):
        to_core(n).wait_send()
    for n in range(3):
        to_plane(n).wait_send()


def shards(wavefunction, left_env, right_env, term_class, sector_sizes, source_table):
    w = lax.axis_index("wf")
    y, z = w // 4, w % 4
    groups = jnp.arange(GROUP, dtype=jnp.int32)
    blocks = source_table.reshape(CLASSES, GROUP, GROUP)
    slot = jnp.sum(jnp.where(blocks // GROUP == w, blocks % GROUP, 0), axis=2)
    here = lax.dynamic_slice_in_dim(source_table, w * GROUP, GROUP, 1) // GROUP
    osrc = ((y - here // 4) % 4) * 4 + (z - here % 4) % 4
    qinv = jnp.sum(jnp.where(osrc[:, None, :] == groups[None, :, None], groups[None, None, :], 0), axis=2)
    bf16, f32, dma = jnp.bfloat16, jnp.float32, pltpu.SemaphoreType.DMA
    smem = pl.BlockSpec(memory_space=pltpu.SMEM)
    anywhere = pl.BlockSpec(memory_space=pl.ANY)
    return pl.pallas_call(
        body,
        out_shape=jax.ShapeDtypeStruct((2, B, B), bf16),
        in_specs=[smem] * 5 + [anywhere] * 3,
        out_specs=pl.BlockSpec(memory_space=pltpu.VMEM),
        scratch_shapes=[pltpu.VMEM((CLASSES, B, B), bf16)] * NO + [
            pltpu.VMEM((GROUP, B, B), bf16),
            pltpu.VMEM((TERMS, GROUP, B, B), bf16),
            pltpu.VMEM((TERMS, GROUP, B, B), bf16),
            pltpu.VMEM((NC, CLASSES, PIECE, B), bf16),
            pltpu.VMEM((NC, CLASSES, PIECE, B), bf16),
            pltpu.VMEM((ND, CLASSES, HALF, B), bf16),
            pltpu.VMEM((TERMS, GROUP, B, B), bf16),
            pltpu.VMEM((4, 2, B, B), f32),
            pltpu.VMEM((4, 2, B, B), f32),
            pltpu.VMEM((4, 2, B, B), f32),
            pltpu.VMEM((3, 2, B, B), bf16),
            pltpu.VMEM((3, 2, B, B), bf16),
            dma((3,)), dma((NC,)), dma((NC,)), dma((NC,)), dma((NC,)), dma((ND,)), dma((ND,)),
            dma((2, NC)), dma((2, NC)), dma((2, NC)), dma((2, NC)), dma((NO,)), dma((NO,)),
            dma((4,)), dma((4,)), dma((3,)), dma((3,)),
        ],
        compiler_params=pltpu.CompilerParams(collective_id=0, has_side_effects=True, vmem_limit_bytes=56 * 2**20),
        cost_estimate=pl.CostEstimate(flops=2 * 2 * TERMS * GROUP * B**3, bytes_accessed=2 * (2 * TERMS + 1) * GROUP * B * B, transcendentals=0),
        name="fetch_multiply_reduce",
    )(slot, qinv, osrc, term_class, sector_sizes, wavefunction, left_env, right_env)


def solution(mesh):
    placed = (
        P("wf", None, None),
        P("env", "wf", None, None),
        P("env", "wf", None, None),
        P("env"),
        P(None, "wf"),
        P(),
    )
    return jax.shard_map(
        shards, mesh=mesh, in_specs=placed, out_specs=P(("wf", "env"), None, None), check_vma=False
    )
```

```python
import jax
import jax.numpy as jnp
from jax import lax
from jax.experimental import pallas as pl
from jax.experimental.pallas import tpu as pltpu
from jax.sharding import PartitionSpec as P

MESH = pl.DeviceIdType.MESH
B = 256
HALF = B // 2
PIECE = HALF // 4
CLASSES = 5
GROUP = 16
TERMS = 4
CHIP = 2 * TERMS

COOP = ((1, 1), (3, 3), (1, 3), (3, 1), (2, 1), (2, 3), (1, 2), (3, 2), (2, 2))
DIRECT = ((0, 1), (0, 3), (1, 0), (3, 0), (0, 2), (2, 0))
OFFSETS = COOP + DIRECT + ((0, 0),)
NC, ND, NO = len(COOP), len(DIRECT), len(COOP) + len(DIRECT)
UNROLL = 8
ORDER = (
    "L0", "L1", "L2", "L3", "L4", "L5", "L6", "L7", "L8", "X0", "T0", "T1", "T2", "T3", "T4", "T5", "D0", "D1", "D2",
    "D3", "D4", "D5", "S0", "S1", "S2", "S3", "F0", "F1", "S4", "A0", "S5", "F2", "A1", "S6", "F3", "A2", "O0", "P0",
    "F4", "S7", "A3", "P1", "F5", "S8", "A4", "E0", "P2", "F6", "A5", "E1", "P3", "P4", "F7", "A6", "E2", "E3", "P5",
    "P9", "F8", "A7", "P6", "P10", "A8", "E4", "E5", "P7", "P11", "P12", "P13", "P14", "P8",
)


def body(index, klass, sizes, wf_hbm, left_hbm, right_hbm, out, *scratch):
    recv = scratch[:NO + 1]
    (wf, left, right, stage_c, stage_d, partial, kept, via_out, via_in, x_out, x_in, kinds_out, kinds_in, kinds,
     load_sem, ss, rs, sq, rq, sd, rd, sx, rx, sf, rf, sc, rc, sv, rv, sr, rr) = scratch[NO + 1:]
    e, w = lax.axis_index("env"), lax.axis_index("wf")
    x, c, y, z = e // 2, e % 2, w // 4, w % 4

    def dev(dx, dc, dy, dz):
        return (((x + dx) % 4) * 2 + (c + dc) % 2, ((y + dy) % 4) * 4 + (z + dz) % 4)

    def remote(src, dst, ssem, rsem, dx, dc, dy, dz):
        return pltpu.make_async_remote_copy(
            src_ref=src, dst_ref=dst, send_sem=ssem, recv_sem=rsem, device_id=dev(dx, dc, dy, dz), device_id_type=MESH)

    load_wf = pltpu.make_async_copy(wf_hbm, wf, load_sem.at[0])
    load_wf.start()
    barrier = pltpu.get_barrier_semaphore()
    partners = [(0, 1, 0, 0), (1, 0, 0, 0), (3, 0, 0, 0)] + [(0, 0, *o) for o in COOP + DIRECT]
    for p in partners:
        pl.semaphore_signal(barrier, inc=1, device_id=dev(*p), device_id_type=MESH)
    load_wf.wait()
    own_terms = pl.ds(c * TERMS, TERMS)
    load_left = pltpu.make_async_copy(left_hbm.at[:, :, c], left.at[own_terms], load_sem.at[1])
    load_right = pltpu.make_async_copy(right_hbm.at[:, :, c], right.at[own_terms], load_sem.at[2])
    load_left.start()
    load_right.start()
    for k in range(TERMS):
        kinds_out[k] = klass[k]
        kinds[c * TERMS + k] = klass[k]

    half = pl.multiple_of(c * HALF, HALF)
    piece = pl.multiple_of(c * HALF + x * PIECE, PIECE)
    prev_piece = pl.multiple_of(c * HALF + ((x + 3) % 4) * PIECE, PIECE)
    next_piece = pl.multiple_of(c * HALF + ((x + 1) % 4) * PIECE, PIECE)
    low = PIECE // 2

    def target(o):
        return ((y + o[0]) % 4) * 4 + (z + o[1]) % 4

    def masked(value, first, q):
        rows = lax.broadcasted_iota(jnp.int32, value.shape, 0) + first
        cols = lax.broadcasted_iota(jnp.int32, value.shape, 1)
        keep = (rows < sizes[0, q]) & (cols < sizes[1, q])
        return jnp.where(keep, value.astype(jnp.float32), 0.0).astype(jnp.bfloat16)

    def stage(dst, o, first, count):
        @pl.loop(0, CLASSES)
        def _(k):
            q = index[0, k, target(o)]
            dst[k] = masked(wf[q, pl.ds(first, count)], first, q)

    def quarter(i):
        return remote(stage_c.at[i], recv[i].at[:, pl.ds(piece, PIECE)], sq.at[i], rq.at[i], 0, 0, *COOP[i])

    def direct(i):
        return remote(stage_d.at[i], recv[NC + i].at[:, pl.ds(half, HALF)], sd.at[i], rd.at[i], 0, 0, *DIRECT[i])

    def share(i, side):
        part = recv[i].at[:, pl.ds(piece, PIECE)]
        return remote(part, part, sx.at[side, i], rx.at[side, i], 1 if side == 0 else 3, 0, 0, 0)

    def forward(i, side):
        first = prev_piece if side == 0 else next_piece + low
        part = recv[i].at[:, pl.ds(pl.multiple_of(first, low), low)]
        return remote(part, part, sf.at[side, i], rf.at[side, i], 1 if side == 0 else 3, 0, 0, 0)

    def across(i):
        part = recv[i].at[:, pl.ds(half, HALF)]
        return remote(part, part, sc.at[i], rc.at[i], 0, 1, 0, 0)

    def swap_env(n):
        src, dst = ((left_hbm, left), (right_hbm, right))[n]
        return remote(src.at[:, :, 1 - c], dst.at[own_terms], ss.at[n], rs.at[n], 0, 1, 0, 0)

    def swap_kinds():
        return remote(kinds_out, kinds_in, ss.at[2], rs.at[2], 0, 1, 0, 0)

    def first_product(i):
        o = OFFSETS[i]
        at = o[0] * 4 + o[1]

        @pl.loop(0, CHIP // UNROLL)
        def _(n):
            for u in range(UNROLL):
                k = n * UNROLL + u
                q = index[1, kinds[k], at]
                got = lax.dot_general(left[k, q // 4, q % 2], recv[i][kinds[k]], (((1,), (0,)), ((), ())), preferred_element_type=jnp.float32)
                partial[k, at] = got.astype(jnp.bfloat16)

    for i in range(NC):
        stage(stage_c.at[i], COOP[i], piece, PIECE)
    pl.semaphore_wait(barrier, len(partners))
    def step_swap(i):
        swap_kinds().start()
        swap_env(0).start()
        swap_env(1).start()

    def step_stage(i):
        stage(stage_d.at[i], DIRECT[i], half, HALF)

    def step_quarter(i):
        quarter(i).start()

    def step_begin(i):
        direct(i).start()

    def step_share(i):
        quarter(i).wait_recv()
        share(i, 0).start()
        share(i, 1).start()

    def step_forward(i):
        for side in (0, 1):
            share(i, side).wait_recv()
            forward(i, side).start()

    def step_across(i):
        for side in (0, 1):
            forward(i, side).wait_recv()
        across(i).start()

    def step_direct(i):
        direct(i).wait_recv()
        across(NC + i).start()

    def step_product(i):
        across(i).wait_recv()
        first_product(i)

    def step_own(i):
        load_left.wait()
        swap_kinds().wait_recv()
        for k in range(TERMS):
            kinds[(1 - c) * TERMS + k] = kinds_in[k]
        swap_env(0).wait_recv()
        stage(recv[NO], (0, 0), 0, B)
        first_product(NO)

    steps = {"L": step_quarter, "X": step_swap, "T": step_stage, "D": step_begin, "S": step_share, "F": step_forward, "A": step_across, "E": step_direct, "P": step_product, "O": step_own}
    for step in ORDER:
        steps[step[0]](int(step[1:]))

    load_right.wait()
    swap_env(1).wait_recv()

    def second_product(g, j):
        q = 4 * g + 2 * c + j
        total = jnp.zeros((B, B), jnp.float32)
        for k in range(CHIP):
            total += lax.dot_general(partial[k, index[2, kinds[k], q]], right[k, g, j], (((1,), (1,)), ((), ())), preferred_element_type=jnp.float32)
        return total

    def via(n):
        return remote(via_out.at[n], via_in.at[n], sv.at[n], rv.at[n], (1, 3)[n], 0, 0, 0)

    def to_plane(n, j):
        return remote(x_out.at[n, j], x_in.at[n, j], sr.at[n, j], rr.at[n, j], (1, 3)[n], 0, 0, 0)

    for n in range(2):
        via_out[n] = second_product((x + 2) % 4, n).astype(jnp.bfloat16)
        via(n).start()
    for n in range(2):
        x_out[n, 1 - n] = second_product((x + (1, 3)[n]) % 4, 1 - n).astype(jnp.bfloat16)
        to_plane(n, 1 - n).start()
    for n in range(2):
        kept[n] = second_product((x + (1, 3)[n]) % 4, n)
    for n in range(2):
        via(n).wait_recv()
        x_out[n, n] = (kept[n] + via_in[n].astype(jnp.float32)).astype(jnp.bfloat16)
        to_plane(n, n).start()
    for j in range(2):
        kept[2 + j] = second_product(x, j)
    for j in range(2):
        total = kept[2 + j]
        for n in (1 - j, j):
            to_plane(n, j).wait_recv()
            total += x_in[n, j].astype(jnp.float32)
        out[j] = masked(total, 0, 4 * x + 2 * c + j)

    for i in range(NC):
        quarter(i).wait_send()
        for side in (0, 1):
            share(i, side).wait_send()
            forward(i, side).wait_send()
    for i in range(ND):
        direct(i).wait_send()
    for i in range(NO):
        across(i).wait_send()
    for n in range(2):
        swap_env(n).wait_send()
    swap_kinds().wait_send()
    for n in range(2):
        via(n).wait_send()
        for j in range(2):
            to_plane(n, j).wait_send()


def shards(wavefunction, left_env, right_env, term_class, sector_sizes, source_table):
    w = lax.axis_index("wf")
    y, z = w // 4, w % 4
    shape = (3, CLASSES, GROUP, GROUP * GROUP)
    what, at, sector = (lax.broadcasted_iota(jnp.int32, shape, n) for n in (0, 2, 3))
    offset = ((y - source_table // 64) % 4) * 4 + (z - source_table // GROUP % 4) % 4
    code = (offset * GROUP + source_table % GROUP)[None, :, None, :]
    offset, place = code // GROUP, code % GROUP
    group, member = sector // GROUP, sector % GROUP
    which = jnp.where(what == 0, (group == at) & (offset == 0), (group == w) & (at == jnp.where(what == 1, offset, member)))
    value = jnp.where(what == 0, place, jnp.where(what == 1, member, offset))
    index = jnp.sum(jnp.where(which, value, 0), axis=3)

    def by_core(env):
        return env.reshape(TERMS, 4, 2, 2, B, B)

    bf16, f32, dma = jnp.bfloat16, jnp.float32, pltpu.SemaphoreType.DMA
    smem = pl.BlockSpec(memory_space=pltpu.SMEM)
    anywhere = pl.BlockSpec(memory_space=pl.ANY)
    return pl.pallas_call(
        body,
        out_shape=jax.ShapeDtypeStruct((2, B, B), bf16),
        in_specs=[smem] * 3 + [anywhere] * 3,
        out_specs=pl.BlockSpec(memory_space=pltpu.VMEM),
        scratch_shapes=[pltpu.VMEM((CLASSES, B, B), bf16)] * (NO + 1) + [
            pltpu.VMEM((GROUP, B, B), bf16),
            pltpu.VMEM((CHIP, 4, 2, B, B), bf16),
            pltpu.VMEM((CHIP, 4, 2, B, B), bf16),
            pltpu.VMEM((NC, CLASSES, PIECE, B), bf16),
            pltpu.VMEM((ND, CLASSES, HALF, B), bf16),
            pltpu.VMEM((CHIP, GROUP, B, B), bf16),
            pltpu.VMEM((4, B, B), f32),
            pltpu.VMEM((2, B, B), bf16),
            pltpu.VMEM((2, B, B), bf16),
            pltpu.VMEM((2, 2, B, B), bf16),
            pltpu.VMEM((2, 2, B, B), bf16),
            pltpu.SMEM((TERMS,), jnp.int32), pltpu.SMEM((TERMS,), jnp.int32), pltpu.SMEM((CHIP,), jnp.int32),
            dma((3,)), dma((3,)), dma((3,)), dma((NC,)), dma((NC,)), dma((ND,)), dma((ND,)),
            dma((2, NC)), dma((2, NC)), dma((2, NC)), dma((2, NC)), dma((NO,)), dma((NO,)),
            dma((2,)), dma((2,)), dma((2, 2)), dma((2, 2)),
        ],
        compiler_params=pltpu.CompilerParams(collective_id=0, has_side_effects=True, vmem_limit_bytes=60 * 2**20),
        cost_estimate=pl.CostEstimate(flops=2 * 2 * TERMS * GROUP * B**3, bytes_accessed=2 * (2 * TERMS + 1) * GROUP * B * B, transcendentals=0),
        name="fetch_multiply_reduce",
    )(index, term_class, sector_sizes, wavefunction, by_core(left_env), by_core(right_env))


def solution(mesh):
    placed = (
        P("wf", None, None),
        P("env", "wf", None, None),
        P("env", "wf", None, None),
        P("env"),
        P(None, "wf"),
        P(),
    )
    return jax.shard_map(
        shards, mesh=mesh, in_specs=placed, out_specs=P(("wf", "env"), None, None), check_vma=False
    )
```

```python
import jax
import jax.numpy as jnp
from jax import lax
from jax.experimental import pallas as pl
from jax.experimental.pallas import tpu as pltpu
from jax.sharding import PartitionSpec as P

MESH = pl.DeviceIdType.MESH
B = 256
HALF = B // 2
PIECE = HALF // 4
CLASSES = 5
GROUP = 16
TERMS = 4
CHIP = 2 * TERMS

PAIR = ((1, 1), (3, 3))
COOP = (None, (1, 3), (3, 1), (2, 1), (2, 3), (1, 2), (3, 2), (2, 2))
DIRECT = ((0, 1), (0, 3), (1, 0), (3, 0), (0, 2), (2, 0), None)
OFFSETS = COOP + DIRECT
NC, ND, NO = len(COOP), len(DIRECT), len(COOP) + len(DIRECT)
ALONE = COOP[1:] + DIRECT[:-1] + ((0, 0),)
UNROLL = 8
EARLY = 1
ORDER = (
    "L0", "L1", "L2", "T6", "D6", "T0", "T1", "T2", "T3", "L3", "L4", "D0", "D1", "L5", "L6", "L7", "D2", "D3", "X0",
    "T4", "T5", "D4", "D5", "S0", "S1", "S2", "F0", "S3", "F1", "A0", "S4", "F2", "A1", "S5", "F3", "A2", "O0", "S6",
    "P1", "F4", "A3", "P2", "S7", "F5", "A4", "E0", "P3", "F6", "A5", "E1", "P4", "F7", "A6", "E2", "E3", "P5", "P8",
    "A7", "P6", "P9", "E4", "E5", "E6", "P10", "P11", "P12", "P13", "Q0", "P7",
)


def body(index, klass, sizes, wf_hbm, left_hbm, right_hbm, out, *scratch):
    fetched = dict(zip(ALONE, scratch))
    (pair, wf, left, right, stage_c, stage_d, partial, kept, via_out, via_in, x_out, x_in, kinds_out, kinds_in, kinds,
     load_sem, ss, rs, sq, rq, sd, rd, sx, rx, sf, rf, sc, rc, sv, rv, sr, rr) = scratch[len(ALONE):]
    e, w = lax.axis_index("env"), lax.axis_index("wf")
    x, c, y, z = e // 2, e % 2, w // 4, w % 4

    def dev(dx, dc, dy, dz):
        return (((x + dx) % 4) * 2 + (c + dc) % 2, ((y + dy) % 4) * 4 + (z + dz) % 4)

    def remote(src, dst, ssem, rsem, dx, dc, dy, dz):
        return pltpu.make_async_remote_copy(
            src_ref=src, dst_ref=dst, send_sem=ssem, recv_sem=rsem, device_id=dev(dx, dc, dy, dz), device_id_type=MESH)

    load_wf = pltpu.make_async_copy(wf_hbm, wf, load_sem.at[0])
    load_wf.start()
    barrier = pltpu.get_barrier_semaphore()
    partners = [(0, 1, 0, 0), (1, 0, 0, 0), (3, 0, 0, 0)] + [(0, 0, *o) for o in ALONE[:-1] + PAIR]
    for p in partners:
        pl.semaphore_signal(barrier, inc=1, device_id=dev(*p), device_id_type=MESH)
    load_wf.wait()
    own_terms = pl.ds(c * TERMS, TERMS)
    load_left = pltpu.make_async_copy(left_hbm.at[:, :, c], left.at[own_terms], load_sem.at[1])
    load_right = pltpu.make_async_copy(right_hbm.at[:, :, c], right.at[own_terms], load_sem.at[2])
    load_left.start()
    load_right.start()
    for k in range(TERMS):
        kinds_out[k] = klass[k]
        kinds[c * TERMS + k] = klass[k]

    half = pl.multiple_of(c * HALF, HALF)
    piece = pl.multiple_of(c * HALF + x * PIECE, PIECE)
    prev_piece = pl.multiple_of(c * HALF + ((x + 3) % 4) * PIECE, PIECE)
    next_piece = pl.multiple_of(c * HALF + ((x + 1) % 4) * PIECE, PIECE)
    low = PIECE // 2

    def offset(i):
        if OFFSETS[i] is None:
            return (1 + 2 * c,) * 2 if i < NC else (3 - 2 * c,) * 2
        return OFFSETS[i]

    def blocks(i):
        if OFFSETS[i] is None:
            return pair.at[c if i < NC else 1 - c]
        return fetched[OFFSETS[i]]

    def target(o):
        return ((y + o[0]) % 4) * 4 + (z + o[1]) % 4

    def masked(value, first, q):
        rows = lax.broadcasted_iota(jnp.int32, value.shape, 0) + first
        cols = lax.broadcasted_iota(jnp.int32, value.shape, 1)
        keep = (rows < sizes[0, q]) & (cols < sizes[1, q])
        return jnp.where(keep, value.astype(jnp.float32), 0.0).astype(jnp.bfloat16)

    def stage(dst, o, first, count):
        @pl.loop(0, CLASSES)
        def _(k):
            q = index[0, k, target(o)]
            dst[k] = masked(wf[q, pl.ds(first, count)], first, q)

    def quarter(i):
        return remote(stage_c.at[i], blocks(i).at[:, pl.ds(piece, PIECE)], sq.at[i], rq.at[i], 0, 0, *offset(i))

    def direct(i):
        return remote(stage_d.at[i], blocks(NC + i).at[:, pl.ds(half, HALF)], sd.at[i], rd.at[i], 0, 0, *offset(NC + i))

    def share(i, side):
        part = blocks(i).at[:, pl.ds(piece, PIECE)]
        return remote(part, part, sx.at[side, i], rx.at[side, i], 1 if side == 0 else 3, 0, 0, 0)

    def forward(i, side):
        first = prev_piece if side == 0 else next_piece + low
        part = blocks(i).at[:, pl.ds(pl.multiple_of(first, low), low)]
        return remote(part, part, sf.at[side, i], rf.at[side, i], 1 if side == 0 else 3, 0, 0, 0)

    def across(i):
        part = blocks(i).at[:, pl.ds(half, HALF)]
        return remote(part, part, sc.at[i], rc.at[i], 0, 1, 0, 0)

    def swap_env(n):
        src, dst = ((left_hbm, left), (right_hbm, right))[n]
        return remote(src.at[:, :, 1 - c], dst.at[own_terms], ss.at[n], rs.at[n], 0, 1, 0, 0)

    def swap_kinds():
        return remote(kinds_out, kinds_in, ss.at[2], rs.at[2], 0, 1, 0, 0)

    def first_product(o, block):
        at = o[0] * 4 + o[1]

        @pl.loop(0, CHIP // UNROLL)
        def _(n):
            for u in range(UNROLL):
                k = n * UNROLL + u
                q = index[1, kinds[k], at]
                got = lax.dot_general(left[k, q // 4, q % 2], block(kinds[k]), (((1,), (0,)), ((), ())), preferred_element_type=jnp.float32)
                partial[k, at] = got.astype(jnp.bfloat16)

    for i in range(EARLY):
        stage(stage_c.at[i], offset(i), piece, PIECE)
    pl.semaphore_wait(barrier, len(partners))
    def step_swap(i):
        swap_kinds().start()
        swap_env(0).start()
        swap_env(1).start()

    def step_stage(i):
        stage(stage_d.at[i], offset(NC + i), half, HALF)

    def step_quarter(i):
        if i >= EARLY:
            stage(stage_c.at[i], offset(i), piece, PIECE)
        quarter(i).start()

    def step_begin(i):
        direct(i).start()

    def step_share(i):
        quarter(i).wait_recv()
        share(i, 0).start()
        share(i, 1).start()

    def step_forward(i):
        for side in (0, 1):
            share(i, side).wait_recv()
            forward(i, side).start()

    def step_across(i):
        for side in (0, 1):
            forward(i, side).wait_recv()
        across(i).start()

    def step_direct(i):
        direct(i).wait_recv()
        across(NC + i).start()

    def step_product(i):
        across(i).wait_recv()
        first_product(OFFSETS[i], lambda k: fetched[OFFSETS[i]][k])

    def step_pair(i):
        across(0).wait_recv()
        across(NO - 1).wait_recv()
        for p in range(2):
            first_product(PAIR[p], lambda k: pair[p, k])

    def step_own(i):
        load_left.wait()
        swap_kinds().wait_recv()
        for k in range(TERMS):
            kinds[(1 - c) * TERMS + k] = kinds_in[k]
        swap_env(0).wait_recv()
        stage(fetched[0, 0], (0, 0), 0, B)
        first_product((0, 0), lambda k: fetched[0, 0][k])

    steps = {"L": step_quarter, "X": step_swap, "T": step_stage, "D": step_begin, "S": step_share, "F": step_forward, "A": step_across, "E": step_direct, "P": step_product, "Q": step_pair, "O": step_own}
    for step in ORDER:
        steps[step[0]](int(step[1:]))

    load_right.wait()
    swap_env(1).wait_recv()

    def second_product(g, j):
        q = 4 * g + 2 * c + j
        total = jnp.zeros((B, B), jnp.float32)
        for k in range(CHIP):
            total += lax.dot_general(partial[k, index[2, kinds[k], q]], right[k, g, j], (((1,), (1,)), ((), ())), preferred_element_type=jnp.float32)
        return total

    def via(n):
        return remote(via_out.at[n], via_in.at[n], sv.at[n], rv.at[n], (1, 3)[n], 0, 0, 0)

    def to_plane(n, j):
        return remote(x_out.at[n, j], x_in.at[n, j], sr.at[n, j], rr.at[n, j], (1, 3)[n], 0, 0, 0)

    for n in range(2):
        via_out[n] = second_product((x + 2) % 4, n).astype(jnp.bfloat16)
        via(n).start()
    for n in range(2):
        x_out[n, 1 - n] = second_product((x + (1, 3)[n]) % 4, 1 - n).astype(jnp.bfloat16)
        to_plane(n, 1 - n).start()
    for n in range(2):
        kept[n] = second_product((x + (1, 3)[n]) % 4, n)
    for n in range(2):
        via(n).wait_recv()
        x_out[n, n] = (kept[n] + via_in[n].astype(jnp.float32)).astype(jnp.bfloat16)
        to_plane(n, n).start()
    for j in range(2):
        kept[2 + j] = second_product(x, j)
    for j in range(2):
        total = kept[2 + j]
        for n in (1 - j, j):
            to_plane(n, j).wait_recv()
            total += x_in[n, j].astype(jnp.float32)
        out[j] = masked(total, 0, 4 * x + 2 * c + j)

    for i in range(NC):
        quarter(i).wait_send()
        for side in (0, 1):
            share(i, side).wait_send()
            forward(i, side).wait_send()
    for i in range(ND):
        direct(i).wait_send()
    for i in range(NO):
        across(i).wait_send()
    for n in range(2):
        swap_env(n).wait_send()
    swap_kinds().wait_send()
    for n in range(2):
        via(n).wait_send()
        for j in range(2):
            to_plane(n, j).wait_send()


def shards(wavefunction, left_env, right_env, term_class, sector_sizes, source_table):
    w = lax.axis_index("wf")
    y, z = w >> 2, w & 3
    shape = (3, CLASSES, GROUP, GROUP * GROUP)
    what, at, sector = (lax.broadcasted_iota(jnp.int32, shape, n) for n in (0, 2, 3))
    offset = (((y - (source_table >> 6)) & 3) << 2) | ((z - (source_table >> 4)) & 3)
    code = ((offset << 4) | (source_table & (GROUP - 1)))[None, :, None, :]
    offset, place = code >> 4, code & (GROUP - 1)
    group, member = sector >> 4, sector & (GROUP - 1)
    which = jnp.where(what == 0, (group == at) & (offset == 0), (group == w) & (at == jnp.where(what == 1, offset, member)))
    value = jnp.where(what == 0, place, jnp.where(what == 1, member, offset))
    index = jnp.sum(jnp.where(which, value, 0), axis=3)

    def by_core(env):
        return env.reshape(TERMS, 4, 2, 2, B, B)

    bf16, f32, dma = jnp.bfloat16, jnp.float32, pltpu.SemaphoreType.DMA
    smem = pl.BlockSpec(memory_space=pltpu.SMEM)
    anywhere = pl.BlockSpec(memory_space=pl.ANY)
    return pl.pallas_call(
        body,
        out_shape=jax.ShapeDtypeStruct((2, B, B), bf16),
        in_specs=[smem] * 3 + [anywhere] * 3,
        out_specs=pl.BlockSpec(memory_space=pltpu.VMEM),
        scratch_shapes=[pltpu.VMEM((CLASSES, B, B), bf16)] * len(ALONE) + [
            pltpu.VMEM((2, CLASSES, B, B), bf16),
            pltpu.VMEM((GROUP, B, B), bf16),
            pltpu.VMEM((CHIP, 4, 2, B, B), bf16),
            pltpu.VMEM((CHIP, 4, 2, B, B), bf16),
            pltpu.VMEM((NC, CLASSES, PIECE, B), bf16),
            pltpu.VMEM((ND, CLASSES, HALF, B), bf16),
            pltpu.VMEM((CHIP, GROUP, B, B), bf16),
            pltpu.VMEM((4, B, B), f32),
            pltpu.VMEM((2, B, B), bf16),
            pltpu.VMEM((2, B, B), bf16),
            pltpu.VMEM((2, 2, B, B), bf16),
            pltpu.VMEM((2, 2, B, B), bf16),
            pltpu.SMEM((TERMS,), jnp.int32), pltpu.SMEM((TERMS,), jnp.int32), pltpu.SMEM((CHIP,), jnp.int32),
            dma((3,)), dma((3,)), dma((3,)), dma((NC,)), dma((NC,)), dma((ND,)), dma((ND,)),
            dma((2, NC)), dma((2, NC)), dma((2, NC)), dma((2, NC)), dma((NO,)), dma((NO,)),
            dma((2,)), dma((2,)), dma((2, 2)), dma((2, 2)),
        ],
        compiler_params=pltpu.CompilerParams(collective_id=0, has_side_effects=True, vmem_limit_bytes=60 * 2**20),
        cost_estimate=pl.CostEstimate(flops=2 * 2 * TERMS * GROUP * B**3, bytes_accessed=2 * (2 * TERMS + 1) * GROUP * B * B, transcendentals=0),
        name="fetch_multiply_reduce",
    )(index, term_class, sector_sizes, wavefunction, by_core(left_env), by_core(right_env))


def solution(mesh):
    placed = (
        P("wf", None, None),
        P("env", "wf", None, None),
        P("env", "wf", None, None),
        P("env"),
        P(None, "wf"),
        P(),
    )
    return jax.shard_map(
        shards, mesh=mesh, in_specs=placed, out_specs=P(("wf", "env"), None, None), check_vma=False
    )
```

```python
import jax
import jax.numpy as jnp
from jax import lax
from jax.experimental import pallas as pl
from jax.experimental.pallas import tpu as pltpu
from jax.sharding import PartitionSpec as P

MESH = pl.DeviceIdType.MESH
B = 256
HALF = B // 2
PIECE = HALF // 4
CLASSES = 5
GROUP = 16
TERMS = 4
CHIP = 2 * TERMS

PAIR = ((1, 1), (3, 3))
COOP = (None, (1, 3), (3, 1), (2, 1), (2, 3), (1, 2), (3, 2), (2, 2))
DIRECT = ((0, 1), (0, 3), (1, 0), (3, 0), (0, 2), (2, 0), None)
OFFSETS = COOP + DIRECT
NC, ND, NO = len(COOP), len(DIRECT), len(COOP) + len(DIRECT)
ALONE = COOP[1:] + DIRECT[:-1] + ((0, 0),)
UNROLL = 8
EARLY = 1
ORDER = (
    "L0", "L1", "L2", "T6", "D6", "T0", "T1", "T2", "T3", "T4", "T5", "L3", "L4", "D0", "D1", "L5", "L6", "L7", "D2",
    "D3", "D4", "D5", "X0", "S0", "S1", "S2", "F0", "S3", "F1", "A0", "S4", "F2", "A1", "S5", "F3", "A2", "O0", "S6",
    "P1", "F4", "A3", "P2", "S7", "F5", "A4", "E0", "P3", "F6", "A5", "E1", "P4", "F7", "A6", "E2", "E3", "P5", "P8",
    "A7", "P6", "P9", "E4", "E5", "E6", "P10", "P11", "P12", "P13", "Q0", "P7",
)


def body(index, klass, sizes, wf_hbm, left_hbm, right_hbm, out, *scratch):
    fetched = dict(zip(ALONE, scratch))
    (pair, wf, left, right, stage_c, stage_d, partial, kept, via_out, via_in, x_out, x_in, kinds_out, kinds_in, kinds,
     load_sem, ss, rs, sq, rq, sd, rd, sx, rx, sf, rf, sc, rc, sv, rv, sr, rr) = scratch[len(ALONE):]
    e, w = lax.axis_index("env"), lax.axis_index("wf")
    x, c, y, z = e // 2, e % 2, w // 4, w % 4

    def dev(dx, dc, dy, dz):
        return (((x + dx) % 4) * 2 + (c + dc) % 2, ((y + dy) % 4) * 4 + (z + dz) % 4)

    def remote(src, dst, ssem, rsem, dx, dc, dy, dz):
        return pltpu.make_async_remote_copy(
            src_ref=src, dst_ref=dst, send_sem=ssem, recv_sem=rsem, device_id=dev(dx, dc, dy, dz), device_id_type=MESH)

    load_wf = pltpu.make_async_copy(wf_hbm, wf, load_sem.at[0])
    load_wf.start()
    barrier = pltpu.get_barrier_semaphore()
    partners = [(0, 1, 0, 0), (1, 0, 0, 0), (3, 0, 0, 0)] + [(0, 0, *o) for o in ALONE[:-1] + PAIR]
    for p in partners:
        pl.semaphore_signal(barrier, inc=1, device_id=dev(*p), device_id_type=MESH)
    load_wf.wait()
    own_terms = pl.ds(c * TERMS, TERMS)
    load_left = pltpu.make_async_copy(left_hbm.at[:, :, c], left.at[own_terms], load_sem.at[1])
    load_right = pltpu.make_async_copy(right_hbm.at[:, :, c], right.at[own_terms], load_sem.at[2])
    load_left.start()
    load_right.start()
    for k in range(TERMS):
        kinds_out[k] = klass[k]
        kinds[c * TERMS + k] = klass[k]

    half = pl.multiple_of(c * HALF, HALF)
    piece = pl.multiple_of(c * HALF + x * PIECE, PIECE)
    prev_piece = pl.multiple_of(c * HALF + ((x + 3) % 4) * PIECE, PIECE)
    next_piece = pl.multiple_of(c * HALF + ((x + 1) % 4) * PIECE, PIECE)
    low = PIECE // 2

    def offset(i):
        if OFFSETS[i] is None:
            return (1 + 2 * c,) * 2 if i < NC else (3 - 2 * c,) * 2
        return OFFSETS[i]

    def blocks(i):
        if OFFSETS[i] is None:
            return pair.at[c if i < NC else 1 - c]
        return fetched[OFFSETS[i]]

    def target(o):
        return ((y + o[0]) % 4) * 4 + (z + o[1]) % 4

    def masked(value, first, q):
        rows = lax.broadcasted_iota(jnp.int32, value.shape, 0) + first
        cols = lax.broadcasted_iota(jnp.int32, value.shape, 1)
        keep = (rows < sizes[0, q]) & (cols < sizes[1, q])
        return jnp.where(keep, value.astype(jnp.float32), 0.0).astype(jnp.bfloat16)

    def stage(dst, o, first, count):
        @pl.loop(0, CLASSES)
        def _(k):
            q = index[0, k, target(o)]
            dst[k] = masked(wf[q, pl.ds(first, count)], first, q)

    def quarter(i):
        return remote(stage_c.at[i], blocks(i).at[:, pl.ds(piece, PIECE)], sq.at[i], rq.at[i], 0, 0, *offset(i))

    def direct(i):
        return remote(stage_d.at[i], blocks(NC + i).at[:, pl.ds(half, HALF)], sd.at[i], rd.at[i], 0, 0, *offset(NC + i))

    def share(i, side):
        part = blocks(i).at[:, pl.ds(piece, PIECE)]
        return remote(part, part, sx.at[side, i], rx.at[side, i], 1 if side == 0 else 3, 0, 0, 0)

    def forward(i, side):
        first = prev_piece if side == 0 else next_piece + low
        part = blocks(i).at[:, pl.ds(pl.multiple_of(first, low), low)]
        return remote(part, part, sf.at[side, i], rf.at[side, i], 1 if side == 0 else 3, 0, 0, 0)

    def across(i):
        part = blocks(i).at[:, pl.ds(half, HALF)]
        return remote(part, part, sc.at[i], rc.at[i], 0, 1, 0, 0)

    def swap_env(n):
        src, dst = ((left_hbm, left), (right_hbm, right))[n]
        return remote(src.at[:, :, 1 - c], dst.at[own_terms], ss.at[n], rs.at[n], 0, 1, 0, 0)

    def swap_kinds():
        return remote(kinds_out, kinds_in, ss.at[2], rs.at[2], 0, 1, 0, 0)

    def first_product(o, block):
        at = o[0] * 4 + o[1]

        @pl.loop(0, CHIP // UNROLL)
        def _(n):
            for u in range(UNROLL):
                k = n * UNROLL + u
                q = index[1, kinds[k], at]
                got = lax.dot_general(left[k, q // 4, q % 2], block(kinds[k]), (((1,), (0,)), ((), ())), preferred_element_type=jnp.float32)
                partial[k, at] = got.astype(jnp.bfloat16)

    for i in range(EARLY):
        stage(stage_c.at[i], offset(i), piece, PIECE)
    pl.semaphore_wait(barrier, len(partners))
    def step_swap(i):
        swap_kinds().start()
        swap_env(0).start()
        swap_env(1).start()

    def step_stage(i):
        stage(stage_d.at[i], offset(NC + i), half, HALF)

    def step_quarter(i):
        if i >= EARLY:
            stage(stage_c.at[i], offset(i), piece, PIECE)
        quarter(i).start()

    def step_begin(i):
        direct(i).start()

    def step_share(i):
        quarter(i).wait_recv()
        share(i, 0).start()
        share(i, 1).start()

    def step_forward(i):
        for side in (0, 1):
            share(i, side).wait_recv()
            forward(i, side).start()

    def step_across(i):
        for side in (0, 1):
            forward(i, side).wait_recv()
        across(i).start()

    def step_direct(i):
        direct(i).wait_recv()
        across(NC + i).start()

    def step_product(i):
        across(i).wait_recv()
        first_product(OFFSETS[i], lambda k: fetched[OFFSETS[i]][k])

    def step_pair(i):
        across(0).wait_recv()
        across(NO - 1).wait_recv()
        for p in range(2):
            first_product(PAIR[p], lambda k: pair[p, k])

    def step_own(i):
        load_left.wait()
        swap_kinds().wait_recv()
        for k in range(TERMS):
            kinds[(1 - c) * TERMS + k] = kinds_in[k]
        swap_env(0).wait_recv()
        stage(fetched[0, 0], (0, 0), 0, B)
        first_product((0, 0), lambda k: fetched[0, 0][k])

    steps = {"L": step_quarter, "X": step_swap, "T": step_stage, "D": step_begin, "S": step_share, "F": step_forward, "A": step_across, "E": step_direct, "P": step_product, "Q": step_pair, "O": step_own}
    for step in ORDER:
        steps[step[0]](int(step[1:]))

    load_right.wait()
    swap_env(1).wait_recv()

    def second_product(g, j):
        q = 4 * g + 2 * c + j
        total = jnp.zeros((B, B), jnp.float32)
        for k in range(CHIP):
            total += lax.dot_general(partial[k, index[2, kinds[k], q]], right[k, g, j], (((1,), (1,)), ((), ())), preferred_element_type=jnp.float32)
        return total

    def via(n):
        return remote(via_out.at[n], via_in.at[n], sv.at[n], rv.at[n], (1, 3)[n], 0, 0, 0)

    def to_plane(n, j):
        return remote(x_out.at[n, j], x_in.at[n, j], sr.at[n, j], rr.at[n, j], (1, 3)[n], 0, 0, 0)

    for n in range(2):
        via_out[n] = second_product((x + 2) % 4, n).astype(jnp.bfloat16)
        via(n).start()
    for n in range(2):
        x_out[n, 1 - n] = second_product((x + (1, 3)[n]) % 4, 1 - n).astype(jnp.bfloat16)
        to_plane(n, 1 - n).start()
    for n in range(2):
        kept[n] = second_product((x + (1, 3)[n]) % 4, n)
    for n in range(2):
        via(n).wait_recv()
        x_out[n, n] = (kept[n] + via_in[n].astype(jnp.float32)).astype(jnp.bfloat16)
        to_plane(n, n).start()
    for j in range(2):
        kept[2 + j] = second_product(x, j)
    for j in range(2):
        total = kept[2 + j]
        for n in (1 - j, j):
            to_plane(n, j).wait_recv()
            total += x_in[n, j].astype(jnp.float32)
        out[j] = masked(total, 0, 4 * x + 2 * c + j)

    for i in range(NC):
        quarter(i).wait_send()
        for side in (0, 1):
            share(i, side).wait_send()
            forward(i, side).wait_send()
    for i in range(ND):
        direct(i).wait_send()
    for i in range(NO):
        across(i).wait_send()
    for n in range(2):
        swap_env(n).wait_send()
    swap_kinds().wait_send()
    for n in range(2):
        via(n).wait_send()
        for j in range(2):
            to_plane(n, j).wait_send()


def shards(wavefunction, left_env, right_env, term_class, sector_sizes, source_table):
    w = lax.axis_index("wf")
    y, z = w // 4, w % 4
    shape = (3, CLASSES, GROUP, GROUP * GROUP)
    what, at, sector = (lax.broadcasted_iota(jnp.int32, shape, n) for n in (0, 2, 3))
    offset = ((y - source_table // 64) % 4) * 4 + (z - source_table // GROUP % 4) % 4
    code = (offset * GROUP + source_table % GROUP)[None, :, None, :]
    offset, place = code // GROUP, code % GROUP
    group, member = sector // GROUP, sector % GROUP
    which = jnp.where(what == 0, (group == at) & (offset == 0), (group == w) & (at == jnp.where(what == 1, offset, member)))
    value = jnp.where(what == 0, place, jnp.where(what == 1, member, offset))
    index = jnp.sum(jnp.where(which, value, 0), axis=3)

    def by_core(env):
        return env.reshape(TERMS, 4, 2, 2, B, B)

    bf16, f32, dma = jnp.bfloat16, jnp.float32, pltpu.SemaphoreType.DMA
    smem = pl.BlockSpec(memory_space=pltpu.SMEM)
    anywhere = pl.BlockSpec(memory_space=pl.ANY)
    return pl.pallas_call(
        body,
        out_shape=jax.ShapeDtypeStruct((2, B, B), bf16),
        in_specs=[smem] * 3 + [anywhere] * 3,
        out_specs=pl.BlockSpec(memory_space=pltpu.VMEM),
        scratch_shapes=[pltpu.VMEM((CLASSES, B, B), bf16)] * len(ALONE) + [
            pltpu.VMEM((2, CLASSES, B, B), bf16),
            pltpu.VMEM((GROUP, B, B), bf16),
            pltpu.VMEM((CHIP, 4, 2, B, B), bf16),
            pltpu.VMEM((CHIP, 4, 2, B, B), bf16),
            pltpu.VMEM((NC, CLASSES, PIECE, B), bf16),
            pltpu.VMEM((ND, CLASSES, HALF, B), bf16),
            pltpu.VMEM((CHIP, GROUP, B, B), bf16),
            pltpu.VMEM((4, B, B), f32),
            pltpu.VMEM((2, B, B), bf16),
            pltpu.VMEM((2, B, B), bf16),
            pltpu.VMEM((2, 2, B, B), bf16),
            pltpu.VMEM((2, 2, B, B), bf16),
            pltpu.SMEM((TERMS,), jnp.int32), pltpu.SMEM((TERMS,), jnp.int32), pltpu.SMEM((CHIP,), jnp.int32),
            dma((3,)), dma((3,)), dma((3,)), dma((NC,)), dma((NC,)), dma((ND,)), dma((ND,)),
            dma((2, NC)), dma((2, NC)), dma((2, NC)), dma((2, NC)), dma((NO,)), dma((NO,)),
            dma((2,)), dma((2,)), dma((2, 2)), dma((2, 2)),
        ],
        compiler_params=pltpu.CompilerParams(collective_id=0, has_side_effects=True, vmem_limit_bytes=60 * 2**20),
        cost_estimate=pl.CostEstimate(flops=2 * 2 * TERMS * GROUP * B**3, bytes_accessed=2 * (2 * TERMS + 1) * GROUP * B * B, transcendentals=0),
        name="fetch_multiply_reduce",
    )(index, term_class, sector_sizes, wavefunction, by_core(left_env), by_core(right_env))


def solution(mesh):
    placed = (
        P("wf", None, None),
        P("env", "wf", None, None),
        P("env", "wf", None, None),
        P("env"),
        P(None, "wf"),
        P(),
    )
    return jax.shard_map(
        shards, mesh=mesh, in_specs=placed, out_specs=P(("wf", "env"), None, None), check_vma=False
    )
```
